32 devices in a mesh: dp: 4 (over x, core), centre: 8 (over z, y).
Axes of the slice: x: 2, y: 2, z: 4, core: 2. Of those that a mesh axis runs over, the one named last changes fastest.
Arguments:
- samples: bfloat16 [16384, 128], P('dp'), may hold values from -24 to 24
- centres: bfloat16 [16384, 128], P('centre'), may hold values from -6 to 6
- facility_prior_logprob: float32 [16384], P('centre'), may hold values from -2 to 0
Outputs:
- new_centres: float32 [16384, 128], P('centre')
- new_log_prior: float32 [16384], P('centre')
- log_partition: float32 [16384], P('dp')
The draws below stay inside these ranges and needn't reach their ends.
All inputs are finite; a program needn't handle non-finite values.
Results may differ from the reference program's by a relative error of at most 0.00075.
Values sent between devices are 32-bit elements; how exact they have to be, the bound alone decides.
A program may use at most 128 MiB of HBM per device.

```python
import jax
import jax.numpy as jnp
from jax import lax

F = 128
K = 16384
NS = 16384


def draw_samples(key, part):
    first = jax.random.fold_in(key, 0)
    fourth = jax.random.fold_in(key, 71)
    fifth = jax.random.fold_in(key, 83)
    values = jax.random.normal(first, (NS, F), jnp.float32)
    reach = jax.random.uniform(fourth, (NS, 1), jnp.float32, 3500.0, 6000.0)
    shift_size = jnp.sqrt(reach / float(F))
    signs = jnp.where(jax.random.uniform(fifth, (NS, 1), jnp.float32) < 0.5, -1.0, 1.0)
    row_index = lax.broadcasted_iota(jnp.int32, (NS, 1), 0)
    far_rows = row_index % 2 == 1
    shifted = jnp.where(far_rows, values + signs * shift_size, values)
    return jnp.clip(shifted, -24.0, 24.0).astype(jnp.bfloat16)


def block_levels(own_key, dims, cuts, least, high):
    loudness, own = 1.0, jax.random.fold_in(own_key, 6)
    for position, shards_of in cuts:
        heights = jnp.exp(jax.random.uniform(jax.random.fold_in(own, position), (shards_of,), jnp.float32, least / len(cuts), high / len(cuts)))
        loudness = loudness * jnp.repeat(heights, dims[position] // shards_of).reshape([-1 if axis == position else 1 for axis in range(len(dims))])
    return loudness


def gaussian(stream_key, dims, spread, limit, shards=(), dtype=jnp.bfloat16):
    gain = block_levels(stream_key, dims, shards, -0.22, 0.18) if shards else 1.0
    array = jax.random.normal(stream_key, dims, jnp.float32) * spread * gain
    return jnp.minimum(jnp.maximum(array, -limit), limit).astype(dtype)


def setup_inputs(seed: int = 0) -> dict:
    streams_of = jax.random.split(jax.random.key(seed), 4)
    samples = draw_samples(jax.random.fold_in(streams_of[3], 71), 0)
    centres = gaussian(streams_of[1], (K, F), 1.0, 6.0, ((0, 8),))
    facility_prior_logprob = jnp.clip(-2.0 + 2.0 * jax.random.uniform(streams_of[2], (K,), jnp.float32) ** block_levels(streams_of[2], (K,), ((0, 8),), -0.2, 0.2), -2.0, 0.0)
    return {"samples": samples, "centres": centres, "facility_prior_logprob": facility_prior_logprob}


inverse_coolness_beta = 0.0625


def reference(samples, centres, facility_prior_logprob):
    centres_wide = centres.astype(jnp.float32)
    facility_norm_sq = jnp.sum(centres_wide * centres_wide, axis=1)
    block_rows = min(512, NS)
    blocks = samples.reshape(NS // block_rows, block_rows, F)

    def block_step(running, rows_block):
        mass, weighted = running
        padded_row_width = rows_block.astype(jnp.float32)
        point_norm_sq = jnp.sum(padded_row_width * padded_row_width, axis=1)
        point_facility_inner = jnp.dot(rows_block, centres.T, preferred_element_type=jnp.float32)
        unnormalised_membership_energy = facility_prior_logprob[None, :] - (point_norm_sq[:, None] - 2.0 * point_facility_inner + facility_norm_sq[None, :]) * inverse_coolness_beta
        row_max = jnp.max(unnormalised_membership_energy, axis=1)
        row_total = jnp.sum(jnp.exp(unnormalised_membership_energy - row_max[:, None]), axis=1)
        partition = row_max + jnp.log(row_total)
        resp = jnp.exp(unnormalised_membership_energy - partition[:, None]).astype(jnp.bfloat16)
        mass = mass + jnp.sum(resp.astype(jnp.float32), axis=0)
        weighted = weighted + jnp.dot(resp.T, rows_block, preferred_element_type=jnp.float32)
        return (mass, weighted), partition

    start = (jnp.zeros((K,), jnp.float32), jnp.zeros((K, F), jnp.float32))
    (mass, weighted), partitions = lax.scan(block_step, start, blocks)
    new_centres = (weighted + centres_wide) / (mass + 1.0)[:, None]
    new_log_prior = jnp.log((mass + 1.0) / float(NS + K))
    return new_centres, new_log_prior, partitions.reshape(NS)
```

```python
import functools

import jax
import jax.numpy as jnp
from jax import lax
from jax.experimental import pallas as pl
from jax.experimental.pallas import tpu as pltpu
from jax.sharding import PartitionSpec as P

MESH = pl.DeviceIdType.MESH
BETA = 0.0625
LANES = 128
COLS = 256
MOST = 256
GROUPS = 2


def pieces(value):
    first = value.astype(jnp.bfloat16)
    rest = value - first.astype(jnp.float32)
    second = rest.astype(jnp.bfloat16)
    third = (rest - second.astype(jnp.float32)).astype(jnp.bfloat16)
    return first, second, third


def side_columns(value):
    lane = lax.broadcasted_iota(jnp.int32, value.shape, 1)
    first, second, third = (p.astype(jnp.float32) for p in pieces(value))
    zero = jnp.zeros_like(value)
    picked = jnp.where(lane == 0, first, jnp.where(lane == 1, second, jnp.where(lane == 2, third, zero)))
    return picked.astype(jnp.bfloat16)


def column(row):
    return jnp.broadcast_to(row, (LANES, LANES)).T


def kernel(
    C, D, x_ref, c_ref, p_ref, out_ref, lp_ref,
    caug, e_ref, xw, score_a, score_b, m_ref, sn_ref, stats, own, send_a, recv_a, recv_b,
    stat_send, stat_recv, a_send, a_recv, b_send, b_recv, c_send, c_recv,
):
    n, k = x_ref.shape[0], c_ref.shape[0]
    X = D // 2
    CHUNK = min(MOST, k // 2)
    H = k // CHUNK // 2
    me_c, me_d = lax.axis_index("centre"), lax.axis_index("dp")
    core, mine_x = lax.rem(me_d, 2), lax.div(me_d, 2)
    sibling = mine_x * 2 + (1 - core)

    def far(q):
        return lax.rem(mine_x + q, X) * 2 + core

    barrier = pltpu.get_barrier_semaphore()

    def greet(q, unused):
        pl.semaphore_signal(
            barrier, inc=1, device_id={"centre": lax.rem(me_c + q, C)}, device_id_type=MESH
        )
        return unused

    lax.fori_loop(1, C, greet, 0)
    pl.semaphore_signal(barrier, inc=1, device_id={"dp": sibling}, device_id_type=MESH)
    for q in range(1, X):
        pl.semaphore_signal(barrier, inc=1, device_id={"dp": far(q)}, device_id_type=MESH)

    def widen(b, unused):
        rows = pl.ds(pl.multiple_of(b * LANES, LANES), LANES)
        c = c_ref[rows, :].astype(jnp.float32)
        norm = jnp.sum(c * c, axis=1, keepdims=True)
        bias = column(p_ref[pl.ds(b, 1), :]) - norm * BETA
        caug[rows, :LANES] = (c * (2.0 * BETA)).astype(jnp.bfloat16)
        caug[rows, LANES:] = side_columns(bias)
        return unused

    lax.fori_loop(0, k // LANES, widen, 0)

    KB = min(512, k)
    steps = n // COLS
    ones = jnp.ones((COLS, LANES), jnp.bfloat16)

    def fold(s, op):
        return op(s.reshape(s.shape[0] // 8, 8, COLS), axis=0)

    def score_block(x_rows, kb):
        return lax.dot_general(
            caug[kb * KB:(kb + 1) * KB, :], x_rows, (((1,), (1,)), ((), ())),
            preferred_element_type=jnp.float32,
        )

    def x_of(j):
        rows = pl.ds(pl.multiple_of(j * COLS, COLS), COLS)
        return jnp.concatenate([x_ref[rows, :], ones], axis=1)

    def first_scores(ref, j):
        xr = x_of(j)
        top = None
        for kb in range(k // KB):
            s = score_block(xr, kb)
            ref[kb * KB:(kb + 1) * KB, :] = s
            part = fold(s, jnp.max)
            top = part if top is None else jnp.maximum(top, part)
        return jnp.max(top, axis=0, keepdims=True)

    def step(now, later, j, m):
        following = jnp.minimum(j + 1, steps - 1)
        xr = x_of(following)
        cols = pl.ds(pl.multiple_of(j * COLS, COLS), COLS)
        top = total = None
        for kb in range(k // KB):
            rows = slice(kb * KB, (kb + 1) * KB)
            s = score_block(xr, kb)
            later[rows, :] = s
            part = fold(s, jnp.max)
            top = part if top is None else jnp.maximum(top, part)
            e = jnp.exp(now[rows, :] - m)
            part = fold(e, jnp.sum)
            total = part if total is None else total + part
            e_ref[rows, cols] = e.astype(jnp.bfloat16)
        lse = m + jnp.log(jnp.sum(total, axis=0, keepdims=True))
        xf = x_ref[cols, :].astype(jnp.float32)
        norm = jnp.sum((xf * xf).T, axis=0, keepdims=True)
        for b in range(COLS // LANES):
            row = pl.ds(j * (COLS // LANES) + b, 1)
            part = slice(b * LANES, (b + 1) * LANES)
            m_ref[row, :] = m[:, part]
            sn_ref[row, :] = norm[:, part]
            stats[0, row, :] = lse[:, part]
        return jnp.max(top, axis=0, keepdims=True)

    def pair(i, m):
        m = step(score_a, score_b, 2 * i, m)
        return step(score_b, score_a, 2 * i + 1, m)

    R = n // LANES
    GR = R // GROUPS

    def stat_copy(g, q):
        rows = slice(g * GR, (g + 1) * GR)
        return pltpu.make_async_remote_copy(
            src_ref=stats.at[0, rows], dst_ref=stats.at[q, rows],
            send_sem=stat_send.at[g, q], recv_sem=stat_recv.at[g, q],
            device_id={"centre": lax.rem(me_c + q, C)}, device_id_type=MESH,
        )

    m = first_scores(score_a, 0)
    per_group = steps // 2 // GROUPS
    for g in range(GROUPS):
        m = lax.fori_loop(g * per_group, (g + 1) * per_group, pair, m)
        if g == 0:
            pl.semaphore_wait(barrier, C - 1 + 1 + X - 1)

        def send(q, unused, g=g):
            stat_copy(g, q).start()
            return unused

        lax.fori_loop(1, C, send, 0)

    for g in range(GROUPS):
        def arrive(q, unused, g=g):
            stat_copy(g, q).wait()
            return unused

        lax.fori_loop(1, C, arrive, 0)
        rows = slice(g * GR, (g + 1) * GR)
        top = lax.fori_loop(
            1, C, lambda q, t, rows=rows: jnp.maximum(t, stats[q, rows, :]), stats[0, rows, :]
        )
        total = lax.fori_loop(
            0, C, lambda q, t, rows=rows, top=top: t + jnp.exp(stats[q, rows, :] - top),
            jnp.zeros_like(top),
        )
        lse = top + jnp.log(total)
        lp_ref[rows, :] = lse - sn_ref[rows, :] * BETA
        m_ref[rows, :] = jnp.exp(m_ref[rows, :] - lse)

        def scale(r, unused):
            at = pl.ds(pl.multiple_of(r * LANES, LANES), LANES)
            w = column(m_ref[pl.ds(r, 1), :])
            xw[at, :LANES] = (x_ref[at, :].astype(jnp.float32) * w).astype(jnp.bfloat16)
            xw[at, LANES:] = side_columns(w)
            return unused

        lax.fori_loop(g * GR, (g + 1) * GR, scale, 0)

    def partial(chunk, ref, i):
        rows = pl.ds(pl.multiple_of(chunk * CHUNK, CHUNK), CHUNK)
        s = jnp.dot(e_ref[rows, :], xw[...], preferred_element_type=jnp.float32)
        ref[i, :CHUNK, :] = s[:, :LANES]
        masses = jnp.zeros((8, LANES), jnp.float32)
        line = lax.broadcasted_iota(jnp.int32, (8, LANES), 0)
        for b in range(CHUNK // LANES):
            t = s[b * LANES:(b + 1) * LANES, LANES:].T
            row = jnp.sum(t[0:8, :], axis=0, keepdims=True)
            masses = jnp.where(line == b, jnp.broadcast_to(row, (8, LANES)), masses)
        ref[i, CHUNK:, :] = masses

    def a_copy(i):
        return pltpu.make_async_remote_copy(
            src_ref=send_a.at[i], dst_ref=recv_a.at[i], send_sem=a_send.at[i], recv_sem=a_recv.at[i],
            device_id={"dp": sibling}, device_id_type=MESH,
        )

    def b_copy(q, i):
        return pltpu.make_async_remote_copy(
            src_ref=own.at[i], dst_ref=recv_b.at[q - 1, i],
            send_sem=b_send.at[q - 1, i], recv_sem=b_recv.at[q - 1, i],
            device_id={"dp": far(q)}, device_id_type=MESH,
        )

    def c_copy(half, i):
        return pltpu.make_async_remote_copy(
            src_ref=out_ref.at[half * H + i], dst_ref=out_ref.at[half * H + i],
            send_sem=c_send.at[i], recv_sem=c_recv.at[i],
            device_id={"dp": sibling}, device_id_type=MESH,
        )

    def chip_sum(i):
        a_copy(i).wait()
        own[i] = own[i] + recv_a[i]
        for q in range(1, X):
            b_copy(q, i).start()

    def produce(i, unused):
        partial((1 - core) * H + i, send_a, i)
        a_copy(i).start()
        partial(core * H + i, own, i)
        chip_sum(i)
        return unused

    lax.fori_loop(0, H, produce, 0)

    denominator = float(n * D + k * C)

    def final(i, unused):
        chunk = core * H + i
        for q in range(1, X):
            b_copy(q, i).wait()
        parts = [own[i]] + [recv_b[q - 1, i] for q in range(1, X)]
        total = functools.reduce(lambda a, b: a + b, parts)
        for b in range(CHUNK // LANES):
            rows = pl.ds(pl.multiple_of(chunk * CHUNK, CHUNK) + b * LANES, LANES)
            mass = column(total[CHUNK + b:CHUNK + b + 1, :])
            c = c_ref[rows, :].astype(jnp.float32)
            out_ref[chunk, b * LANES:(b + 1) * LANES, :] = (
                total[b * LANES:(b + 1) * LANES, :] + c
            ) / (mass + 1.0)
        out_ref[chunk, CHUNK:, :] = jnp.log((total[CHUNK:, :] + 1.0) / denominator)
        c_copy(core, i).start()
        return unused

    lax.fori_loop(0, H, final, 0)

    def finish(i, unused):
        c_copy(core, i).wait()
        return unused

    lax.fori_loop(0, H, finish, 0)


def solution(mesh):
    C, D = mesh.shape["centre"], mesh.shape["dp"]

    def shards(samples, centres, prior):
        n, k = samples.shape[0], centres.shape[0]
        CHUNK = min(MOST, k // 2)
        X, H, R = D // 2, k // CHUNK // 2, n // LANES
        vmem = pl.BlockSpec(memory_space=pltpu.VMEM)
        f32, bf16 = jnp.float32, jnp.bfloat16
        dma = pltpu.SemaphoreType.DMA
        chunk = (CHUNK + 8, LANES)
        out, lp = pl.pallas_call(
            functools.partial(kernel, C, D),
            out_shape=(
                jax.ShapeDtypeStruct((2 * H,) + chunk, f32),
                jax.ShapeDtypeStruct((R, LANES), f32),
            ),
            in_specs=[vmem] * 3,
            out_specs=(vmem, vmem),
            scratch_shapes=[
                pltpu.VMEM((k, 2 * LANES), bf16),
                pltpu.VMEM((k, n), bf16),
                pltpu.VMEM((n, 2 * LANES), bf16),
                pltpu.VMEM((k, COLS), f32),
                pltpu.VMEM((k, COLS), f32),
                pltpu.VMEM((R, LANES), f32),
                pltpu.VMEM((R, LANES), f32),
                pltpu.VMEM((C, R, LANES), f32),
                pltpu.VMEM((H,) + chunk, f32),
                pltpu.VMEM((H,) + chunk, f32),
                pltpu.VMEM((H,) + chunk, f32),
                pltpu.VMEM((max(X - 1, 1), H) + chunk, f32),
                dma((GROUPS, C)), dma((GROUPS, C)),
                dma((H,)), dma((H,)),
                dma((max(X - 1, 1), H)), dma((max(X - 1, 1), H)),
                dma((H,)), dma((H,)),
            ],
            compiler_params=pltpu.CompilerParams(
                collective_id=0, has_side_effects=True, vmem_limit_bytes=50 * 2**20
            ),
            cost_estimate=pl.CostEstimate(
                flops=8 * n * k * LANES, bytes_accessed=4 * n * LANES, transcendentals=n * k
            ),
        )(samples, centres, prior.reshape(k // LANES, LANES))
        new_centres = out[:, :CHUNK, :].reshape(k, LANES)
        new_log_prior = out[:, CHUNK:CHUNK + CHUNK // LANES, :].reshape(k)
        return new_centres, new_log_prior, lp.reshape(n)

    return jax.shard_map(
        shards,
        mesh=mesh,
        in_specs=(P("dp", None), P("centre", None), P("centre")),
        out_specs=(P("centre", None), P("centre"), P("dp")),
        check_vma=False,
    )
```

```python
import functools
import math

import jax
import jax.numpy as jnp
from jax import lax
from jax.experimental import pallas as pl
from jax.experimental.pallas import tpu as pltpu
from jax.sharding import PartitionSpec as P

MESH = pl.DeviceIdType.MESH
BETA = 0.0625
LANES = 128
COLS = 256
MOST = 256
GROUPS = 2


def pieces(value):
    first = value.astype(jnp.bfloat16)
    rest = value - first.astype(jnp.float32)
    second = rest.astype(jnp.bfloat16)
    third = (rest - second.astype(jnp.float32)).astype(jnp.bfloat16)
    return first, second, third


def side_columns(row):
    first, second, third = (p.astype(jnp.float32) for p in pieces(jnp.broadcast_to(row, (8, LANES))))
    line = lax.broadcasted_iota(jnp.int32, (8, LANES), 0)
    zero = jnp.zeros_like(first)
    eight = jnp.where(line == 0, first, jnp.where(line == 1, second, jnp.where(line == 2, third, zero)))
    rest = jnp.zeros((LANES - 8, LANES), jnp.float32)
    return jnp.concatenate([eight, rest], axis=0).T.astype(jnp.bfloat16)


def column(row):
    return jnp.broadcast_to(row, (LANES, LANES)).T


def unrolled(start, stop, body, most=4):
    width = math.gcd(stop - start, most)

    def step(i, unused):
        for u in range(width):
            body(start + i * width + u)
        return unused

    lax.fori_loop(0, (stop - start) // width, step, 0)


def kernel(
    C, D, x_hbm, c_hbm, p_hbm, out_ref, lp_ref, x_ref, c_ref, p_ref, in_sem,
    caug, e_ref, xw, score_a, score_b, m_ref, sn_ref, stats, own, send_a, recv_a, recv_b,
    stat_send, stat_recv, a_send, a_recv, b_send, b_recv, c_send, c_recv,
):
    n, k = x_ref.shape[0], c_ref.shape[0]
    X = D // 2
    CHUNK = min(MOST, k // 2)
    H = k // CHUNK // 2
    me_c, me_d = lax.axis_index("centre"), lax.axis_index("dp")
    core, mine_x = lax.rem(me_d, 2), lax.div(me_d, 2)
    sibling = mine_x * 2 + (1 - core)

    def far(q):
        return lax.rem(mine_x + q, X) * 2 + core

    p_copy = pltpu.make_async_copy(p_hbm, p_ref, in_sem.at[0])
    c_copy_in = pltpu.make_async_copy(c_hbm, c_ref, in_sem.at[1])
    x_copy = pltpu.make_async_copy(x_hbm, x_ref, in_sem.at[2])
    for copy in (p_copy, c_copy_in, x_copy):
        copy.start()

    barrier = pltpu.get_barrier_semaphore()

    def greet(q, unused):
        pl.semaphore_signal(
            barrier, inc=1, device_id={"centre": lax.rem(me_c + q, C)}, device_id_type=MESH
        )
        return unused

    lax.fori_loop(1, C, greet, 0)
    pl.semaphore_signal(barrier, inc=1, device_id={"dp": sibling}, device_id_type=MESH)
    for q in range(1, X):
        pl.semaphore_signal(barrier, inc=1, device_id={"dp": far(q)}, device_id_type=MESH)

    def widen(b):
        rows = pl.ds(pl.multiple_of(b * LANES, LANES), LANES)
        c = c_ref[rows, :].astype(jnp.float32)
        norm = jnp.sum((c * c).T, axis=0, keepdims=True)
        caug[rows, :LANES] = (c * (2.0 * BETA)).astype(jnp.bfloat16)
        caug[rows, LANES:] = side_columns(p_ref[pl.ds(b, 1), :] - norm * BETA)

    p_copy.wait()
    c_copy_in.wait()
    unrolled(0, k // LANES, widen)
    x_copy.wait()

    KB = min(512, k)
    steps = n // COLS
    ones = jnp.ones((COLS, LANES), jnp.bfloat16)

    def fold(s, op):
        return op(s.reshape(s.shape[0] // 8, 8, COLS), axis=0)

    def score_block(x_rows, kb):
        return lax.dot_general(
            caug[kb * KB:(kb + 1) * KB, :], x_rows, (((1,), (1,)), ((), ())),
            preferred_element_type=jnp.float32,
        )

    def x_of(j):
        rows = pl.ds(pl.multiple_of(j * COLS, COLS), COLS)
        return jnp.concatenate([x_ref[rows, :], ones], axis=1)

    def first_scores(ref, j):
        xr = x_of(j)
        top = None
        for kb in range(k // KB):
            s = score_block(xr, kb)
            ref[kb * KB:(kb + 1) * KB, :] = s
            part = fold(s, jnp.max)
            top = part if top is None else jnp.maximum(top, part)
        return jnp.max(top, axis=0, keepdims=True)

    def step(now, later, j, m):
        following = jnp.minimum(j + 1, steps - 1)
        xr = x_of(following)
        cols = pl.ds(pl.multiple_of(j * COLS, COLS), COLS)
        top = total = None
        for kb in range(k // KB):
            rows = slice(kb * KB, (kb + 1) * KB)
            s = score_block(xr, kb)
            later[rows, :] = s
            part = fold(s, jnp.max)
            top = part if top is None else jnp.maximum(top, part)
            e = jnp.exp(now[rows, :] - m)
            part = fold(e, jnp.sum)
            total = part if total is None else total + part
            e_ref[rows, cols] = e.astype(jnp.bfloat16)
        lse = m + jnp.log(jnp.sum(total, axis=0, keepdims=True))
        xf = x_ref[cols, :].astype(jnp.float32)
        norm = jnp.sum((xf * xf).T, axis=0, keepdims=True)
        for b in range(COLS // LANES):
            row = pl.ds(j * (COLS // LANES) + b, 1)
            part = slice(b * LANES, (b + 1) * LANES)
            m_ref[row, :] = m[:, part]
            sn_ref[row, :] = norm[:, part]
            stats[0, row, :] = lse[:, part]
        return jnp.max(top, axis=0, keepdims=True)

    def pair(i, m):
        m = step(score_a, score_b, 2 * i, m)
        return step(score_b, score_a, 2 * i + 1, m)

    R = n // LANES
    GR = R // GROUPS

    def stat_copy(g, q):
        rows = slice(g * GR, (g + 1) * GR)
        return pltpu.make_async_remote_copy(
            src_ref=stats.at[0, rows], dst_ref=stats.at[q, rows],
            send_sem=stat_send.at[g, q], recv_sem=stat_recv.at[g, q],
            device_id={"centre": lax.rem(me_c + q, C)}, device_id_type=MESH,
        )

    m = first_scores(score_a, 0)
    per_group = steps // 2 // GROUPS
    for g in range(GROUPS):
        m = lax.fori_loop(g * per_group, (g + 1) * per_group, pair, m)
        if g == 0:
            pl.semaphore_wait(barrier, C - 1 + 1 + X - 1)

        def send(q, unused, g=g):
            stat_copy(g, q).start()
            return unused

        lax.fori_loop(1, C, send, 0)

    for g in range(GROUPS):
        def arrive(q, unused, g=g):
            stat_copy(g, q).wait()
            return unused

        lax.fori_loop(1, C, arrive, 0)
        rows = slice(g * GR, (g + 1) * GR)
        top = lax.fori_loop(
            1, C, lambda q, t, rows=rows: jnp.maximum(t, stats[q, rows, :]), stats[0, rows, :]
        )
        total = lax.fori_loop(
            0, C, lambda q, t, rows=rows, top=top: t + jnp.exp(stats[q, rows, :] - top),
            jnp.zeros_like(top),
        )
        lse = top + jnp.log(total)
        lp_ref[rows, :] = lse - sn_ref[rows, :] * BETA
        m_ref[rows, :] = jnp.exp(m_ref[rows, :] - lse)

        def scale(r):
            at = pl.ds(pl.multiple_of(r * LANES, LANES), LANES)
            w = column(m_ref[pl.ds(r, 1), :])
            xw[at, :LANES] = (x_ref[at, :].astype(jnp.float32) * w).astype(jnp.bfloat16)
            xw[at, LANES:] = side_columns(m_ref[pl.ds(r, 1), :])

        unrolled(g * GR, (g + 1) * GR, scale)

    def partial(i):
        theirs, mine = (
            e_ref[pl.ds(pl.multiple_of((half * H + i) * CHUNK, CHUNK), CHUNK), :] for half in (1 - core, core)
        )
        both = jnp.dot(
            jnp.concatenate([theirs, mine], axis=0), xw[...], preferred_element_type=jnp.float32
        )
        line = lax.broadcasted_iota(jnp.int32, (8, LANES), 0)
        for ref, s in ((send_a, both[:CHUNK]), (own, both[CHUNK:])):
            ref[i, :CHUNK, :] = s[:, :LANES]
            masses = jnp.zeros((8, LANES), jnp.float32)
            for b in range(CHUNK // LANES):
                t = s[b * LANES:(b + 1) * LANES, LANES:].T
                row = jnp.sum(t[0:8, :], axis=0, keepdims=True)
                masses = jnp.where(line == b, jnp.broadcast_to(row, (8, LANES)), masses)
            ref[i, CHUNK:, :] = masses

    def a_copy(i):
        return pltpu.make_async_remote_copy(
            src_ref=send_a.at[i], dst_ref=recv_a.at[i], send_sem=a_send.at[i], recv_sem=a_recv.at[i],
            device_id={"dp": sibling}, device_id_type=MESH,
        )

    def b_copy(q, i):
        return pltpu.make_async_remote_copy(
            src_ref=own.at[i], dst_ref=recv_b.at[q - 1, i],
            send_sem=b_send.at[q - 1, i], recv_sem=b_recv.at[q - 1, i],
            device_id={"dp": far(q)}, device_id_type=MESH,
        )

    def c_copy(half, i):
        return pltpu.make_async_remote_copy(
            src_ref=out_ref.at[half * H + i], dst_ref=out_ref.at[half * H + i],
            send_sem=c_send.at[i], recv_sem=c_recv.at[i],
            device_id={"dp": sibling}, device_id_type=MESH,
        )

    def chip_sum(i):
        a_copy(i).wait()
        own[i] = own[i] + recv_a[i]
        for q in range(1, X):
            b_copy(q, i).start()

    def produce(i, unused):
        partial(i)
        a_copy(i).start()
        chip_sum(i)
        return unused

    lax.fori_loop(0, H, produce, 0)

    denominator = float(n * D + k * C)

    def final(i, unused):
        chunk = core * H + i
        for q in range(1, X):
            b_copy(q, i).wait()
        parts = [own[i]] + [recv_b[q - 1, i] for q in range(1, X)]
        total = functools.reduce(lambda a, b: a + b, parts)
        for b in range(CHUNK // LANES):
            rows = pl.ds(pl.multiple_of(chunk * CHUNK, CHUNK) + b * LANES, LANES)
            mass = column(total[CHUNK + b:CHUNK + b + 1, :])
            c = c_ref[rows, :].astype(jnp.float32)
            out_ref[chunk, b * LANES:(b + 1) * LANES, :] = (
                total[b * LANES:(b + 1) * LANES, :] + c
            ) / (mass + 1.0)
        out_ref[chunk, CHUNK:, :] = jnp.log((total[CHUNK:, :] + 1.0) / denominator)
        c_copy(core, i).start()
        return unused

    lax.fori_loop(0, H, final, 0)

    def finish(i, unused):
        c_copy(core, i).wait()
        return unused

    lax.fori_loop(0, H, finish, 0)


def solution(mesh):
    C, D = mesh.shape["centre"], mesh.shape["dp"]

    def shards(samples, centres, prior):
        n, k = samples.shape[0], centres.shape[0]
        CHUNK = min(MOST, k // 2)
        X, H, R = D // 2, k // CHUNK // 2, n // LANES
        vmem = pl.BlockSpec(memory_space=pltpu.VMEM)
        f32, bf16 = jnp.float32, jnp.bfloat16
        dma = pltpu.SemaphoreType.DMA
        chunk = (CHUNK + 8, LANES)
        out, lp = pl.pallas_call(
            functools.partial(kernel, C, D),
            out_shape=(
                jax.ShapeDtypeStruct((2 * H,) + chunk, f32),
                jax.ShapeDtypeStruct((R, LANES), f32),
            ),
            in_specs=[pl.BlockSpec(memory_space=pltpu.HBM)] * 3,
            out_specs=(vmem, vmem),
            scratch_shapes=[
                pltpu.VMEM((n, LANES), bf16),
                pltpu.VMEM((k, LANES), bf16),
                pltpu.VMEM((k // LANES, LANES), f32),
                dma((3,)),
                pltpu.VMEM((k, 2 * LANES), bf16),
                pltpu.VMEM((k, n), bf16),
                pltpu.VMEM((n, 2 * LANES), bf16),
                pltpu.VMEM((k, COLS), f32),
                pltpu.VMEM((k, COLS), f32),
                pltpu.VMEM((R, LANES), f32),
                pltpu.VMEM((R, LANES), f32),
                pltpu.VMEM((C, R, LANES), f32),
                pltpu.VMEM((H,) + chunk, f32),
                pltpu.VMEM((H,) + chunk, f32),
                pltpu.VMEM((H,) + chunk, f32),
                pltpu.VMEM((max(X - 1, 1), H) + chunk, f32),
                dma((GROUPS, C)), dma((GROUPS, C)),
                dma((H,)), dma((H,)),
                dma((max(X - 1, 1), H)), dma((max(X - 1, 1), H)),
                dma((H,)), dma((H,)),
            ],
            compiler_params=pltpu.CompilerParams(
                collective_id=0, has_side_effects=True, vmem_limit_bytes=50 * 2**20
            ),
            cost_estimate=pl.CostEstimate(
                flops=8 * n * k * LANES, bytes_accessed=4 * n * LANES, transcendentals=n * k
            ),
        )(samples, centres, prior.reshape(k // LANES, LANES))
        new_centres = out[:, :CHUNK, :].reshape(k, LANES)
        new_log_prior = out[:, CHUNK:CHUNK + CHUNK // LANES, :].reshape(k)
        return new_centres, new_log_prior, lp.reshape(n)

    return jax.shard_map(
        shards,
        mesh=mesh,
        in_specs=(P("dp", None), P("centre", None), P("centre")),
        out_specs=(P("centre", None), P("centre"), P("dp")),
        check_vma=False,
    )
```

```python
import functools
import math

import jax
import jax.numpy as jnp
from jax import lax
from jax.experimental import pallas as pl
from jax.experimental.pallas import tpu as pltpu
from jax.sharding import PartitionSpec as P

MESH = pl.DeviceIdType.MESH
BETA = 0.0625
LANES = 128
COLS = 256
MOST = 256
GROUPS = 4


def pieces(value):
    first = value.astype(jnp.bfloat16)
    rest = value - first.astype(jnp.float32)
    second = rest.astype(jnp.bfloat16)
    third = (rest - second.astype(jnp.float32)).astype(jnp.bfloat16)
    return first, second, third


def side_columns(row):
    first, second, third = (p.astype(jnp.float32) for p in pieces(jnp.broadcast_to(row, (8, LANES))))
    line = lax.broadcasted_iota(jnp.int32, (8, LANES), 0)
    zero = jnp.zeros_like(first)
    eight = jnp.where(line == 0, first, jnp.where(line == 1, second, jnp.where(line == 2, third, zero)))
    rest = jnp.zeros((LANES - 8, LANES), jnp.float32)
    return jnp.concatenate([eight, rest], axis=0).T.astype(jnp.bfloat16)


def column(row):
    return jnp.broadcast_to(row, (LANES, LANES)).T


def unrolled(start, stop, body, most=4):
    width = math.gcd(stop - start, most)

    def step(i, unused):
        for u in range(width):
            body(start + i * width + u)
        return unused

    lax.fori_loop(0, (stop - start) // width, step, 0)


def kernel(
    C, D, x_hbm, c_hbm, p_hbm, out_ref, lp_ref, x_ref, c_ref, p_ref, in_sem,
    caug, e_ref, xw, score_a, score_b, m_ref, sn_ref, stats, own, send_a, recv_a, recv_b,
    stat_send, stat_recv, a_send, a_recv, b_send, b_recv, c_send, c_recv,
):
    n, k = x_ref.shape[0], c_ref.shape[0]
    X = D // 2
    CHUNK = min(MOST, k // 2)
    H = k // CHUNK // 2
    me_c, me_d = lax.axis_index("centre"), lax.axis_index("dp")
    core, mine_x = lax.rem(me_d, 2), lax.div(me_d, 2)
    sibling = mine_x * 2 + (1 - core)

    def far(q):
        return lax.rem(mine_x + q, X) * 2 + core

    p_copy = pltpu.make_async_copy(p_hbm, p_ref, in_sem.at[0])
    c_copy_in = pltpu.make_async_copy(c_hbm, c_ref, in_sem.at[1])
    x_copy = pltpu.make_async_copy(x_hbm, x_ref, in_sem.at[2])
    for copy in (p_copy, c_copy_in, x_copy):
        copy.start()

    barrier = pltpu.get_barrier_semaphore()

    def greet(q, unused):
        pl.semaphore_signal(
            barrier, inc=1, device_id={"centre": lax.rem(me_c + q, C)}, device_id_type=MESH
        )
        return unused

    lax.fori_loop(1, C, greet, 0)
    pl.semaphore_signal(barrier, inc=1, device_id={"dp": sibling}, device_id_type=MESH)
    for q in range(1, X):
        pl.semaphore_signal(barrier, inc=1, device_id={"dp": far(q)}, device_id_type=MESH)

    def widen(b):
        rows = pl.ds(pl.multiple_of(b * LANES, LANES), LANES)
        c = c_ref[rows, :].astype(jnp.float32)
        norm = jnp.sum((c * c).T, axis=0, keepdims=True)
        caug[rows, :LANES] = (c * (2.0 * BETA)).astype(jnp.bfloat16)
        caug[rows, LANES:] = side_columns(p_ref[pl.ds(b, 1), :] - norm * BETA)

    p_copy.wait()
    c_copy_in.wait()
    unrolled(0, k // LANES, widen)
    x_copy.wait()

    KB = min(512, k)
    steps = n // COLS
    ones = jnp.ones((COLS, LANES), jnp.bfloat16)

    def fold(s, op):
        return op(s.reshape(s.shape[0] // 8, 8, COLS), axis=0)

    def score_block(x_rows, kb):
        return lax.dot_general(
            caug[kb * KB:(kb + 1) * KB, :], x_rows, (((1,), (1,)), ((), ())),
            preferred_element_type=jnp.float32,
        )

    def x_of(j):
        rows = pl.ds(pl.multiple_of(j * COLS, COLS), COLS)
        return jnp.concatenate([x_ref[rows, :], ones], axis=1)

    def first_scores(ref, j):
        xr = x_of(j)
        top = None
        for kb in range(k // KB):
            s = score_block(xr, kb)
            ref[kb * KB:(kb + 1) * KB, :] = s
            part = fold(s, jnp.max)
            top = part if top is None else jnp.maximum(top, part)
        return jnp.max(top, axis=0, keepdims=True)

    def step(now, later, j, m):
        following = jnp.minimum(j + 1, steps - 1)
        xr = x_of(following)
        cols = pl.ds(pl.multiple_of(j * COLS, COLS), COLS)
        top = total = None
        for kb in range(k // KB):
            rows = slice(kb * KB, (kb + 1) * KB)
            s = score_block(xr, kb)
            later[rows, :] = s
            part = fold(s, jnp.max)
            top = part if top is None else jnp.maximum(top, part)
            e = jnp.exp(now[rows, :] - m)
            part = fold(e, jnp.sum)
            total = part if total is None else total + part
            e_ref[rows, cols] = e.astype(jnp.bfloat16)
        lse = m + jnp.log(jnp.sum(total, axis=0, keepdims=True))
        xf = x_ref[cols, :].astype(jnp.float32)
        norm = jnp.sum((xf * xf).T, axis=0, keepdims=True)
        for b in range(COLS // LANES):
            row = pl.ds(j * (COLS // LANES) + b, 1)
            part = slice(b * LANES, (b + 1) * LANES)
            m_ref[row, :] = m[:, part]
            sn_ref[row, :] = norm[:, part]
            stats[0, row, :] = lse[:, part]
        return jnp.max(top, axis=0, keepdims=True)

    def pair(i, m):
        m = step(score_a, score_b, 2 * i, m)
        return step(score_b, score_a, 2 * i + 1, m)

    R = n // LANES
    GR = R // GROUPS

    def stat_copy(g, q):
        rows = slice(g * GR, (g + 1) * GR)
        return pltpu.make_async_remote_copy(
            src_ref=stats.at[0, rows], dst_ref=stats.at[q, rows],
            send_sem=stat_send.at[g, q], recv_sem=stat_recv.at[g, q],
            device_id={"centre": lax.rem(me_c + q, C)}, device_id_type=MESH,
        )

    m = first_scores(score_a, 0)
    per_group = steps // 2 // GROUPS
    for g in range(GROUPS):
        m = lax.fori_loop(g * per_group, (g + 1) * per_group, pair, m)
        if g == 0:
            pl.semaphore_wait(barrier, C - 1 + 1 + X - 1)

        def send(q, unused, g=g):
            stat_copy(g, q).start()
            return unused

        lax.fori_loop(1, C, send, 0)

    for g in range(GROUPS):
        def arrive(q, unused, g=g):
            stat_copy(g, q).wait()
            return unused

        lax.fori_loop(1, C, arrive, 0)
        rows = slice(g * GR, (g + 1) * GR)
        top = lax.fori_loop(
            1, C, lambda q, t, rows=rows: jnp.maximum(t, stats[q, rows, :]), stats[0, rows, :]
        )
        total = lax.fori_loop(
            0, C, lambda q, t, rows=rows, top=top: t + jnp.exp(stats[q, rows, :] - top),
            jnp.zeros_like(top),
        )
        lse = top + jnp.log(total)
        lp_ref[rows, :] = lse - sn_ref[rows, :] * BETA
        m_ref[rows, :] = jnp.exp(m_ref[rows, :] - lse)

        def scale(r):
            at = pl.ds(pl.multiple_of(r * LANES, LANES), LANES)
            w = column(m_ref[pl.ds(r, 1), :])
            xw[at, :LANES] = (x_ref[at, :].astype(jnp.float32) * w).astype(jnp.bfloat16)
            xw[at, LANES:] = side_columns(m_ref[pl.ds(r, 1), :])

        unrolled(g * GR, (g + 1) * GR, scale)

    def partial(i):
        theirs, mine = (
            e_ref[pl.ds(pl.multiple_of((half * H + i) * CHUNK, CHUNK), CHUNK), :] for half in (1 - core, core)
        )
        both = jnp.dot(
            jnp.concatenate([theirs, mine], axis=0), xw[...], preferred_element_type=jnp.float32
        )
        line = lax.broadcasted_iota(jnp.int32, (8, LANES), 0)
        for ref, s in ((send_a, both[:CHUNK]), (own, both[CHUNK:])):
            ref[i, :CHUNK, :] = s[:, :LANES]
            masses = jnp.zeros((8, LANES), jnp.float32)
            for b in range(CHUNK // LANES):
                t = s[b * LANES:(b + 1) * LANES, LANES:].T
                row = jnp.sum(t[0:8, :], axis=0, keepdims=True)
                masses = jnp.where(line == b, jnp.broadcast_to(row, (8, LANES)), masses)
            ref[i, CHUNK:, :] = masses

    def a_copy(i):
        return pltpu.make_async_remote_copy(
            src_ref=send_a.at[i], dst_ref=recv_a.at[i], send_sem=a_send.at[i], recv_sem=a_recv.at[i],
            device_id={"dp": sibling}, device_id_type=MESH,
        )

    def b_copy(q, i):
        return pltpu.make_async_remote_copy(
            src_ref=own.at[i], dst_ref=recv_b.at[q - 1, i],
            send_sem=b_send.at[q - 1, i], recv_sem=b_recv.at[q - 1, i],
            device_id={"dp": far(q)}, device_id_type=MESH,
        )

    def c_copy(half, i):
        return pltpu.make_async_remote_copy(
            src_ref=out_ref.at[half * H + i], dst_ref=out_ref.at[half * H + i],
            send_sem=c_send.at[i], recv_sem=c_recv.at[i],
            device_id={"dp": sibling}, device_id_type=MESH,
        )

    def chip_sum(i):
        a_copy(i).wait()
        own[i] = own[i] + recv_a[i]
        for q in range(1, X):
            b_copy(q, i).start()

    def produce(i, unused):
        partial(i)
        a_copy(i).start()
        chip_sum(i)
        return unused

    lax.fori_loop(0, H, produce, 0)

    denominator = float(n * D + k * C)

    def final(i, unused):
        chunk = core * H + i
        for q in range(1, X):
            b_copy(q, i).wait()
        parts = [own[i]] + [recv_b[q - 1, i] for q in range(1, X)]
        total = functools.reduce(lambda a, b: a + b, parts)
        for b in range(CHUNK // LANES):
            rows = pl.ds(pl.multiple_of(chunk * CHUNK, CHUNK) + b * LANES, LANES)
            mass = column(total[CHUNK + b:CHUNK + b + 1, :])
            c = c_ref[rows, :].astype(jnp.float32)
            out_ref[chunk, b * LANES:(b + 1) * LANES, :] = (
                total[b * LANES:(b + 1) * LANES, :] + c
            ) / (mass + 1.0)
        out_ref[chunk, CHUNK:, :] = jnp.log((total[CHUNK:, :] + 1.0) / denominator)
        c_copy(core, i).start()
        return unused

    lax.fori_loop(0, H, final, 0)

    def finish(i, unused):
        c_copy(core, i).wait()
        return unused

    lax.fori_loop(0, H, finish, 0)


def solution(mesh):
    C, D = mesh.shape["centre"], mesh.shape["dp"]

    def shards(samples, centres, prior):
        n, k = samples.shape[0], centres.shape[0]
        CHUNK = min(MOST, k // 2)
        X, H, R = D // 2, k // CHUNK // 2, n // LANES
        vmem = pl.BlockSpec(memory_space=pltpu.VMEM)
        f32, bf16 = jnp.float32, jnp.bfloat16
        dma = pltpu.SemaphoreType.DMA
        chunk = (CHUNK + 8, LANES)
        out, lp = pl.pallas_call(
            functools.partial(kernel, C, D),
            out_shape=(
                jax.ShapeDtypeStruct((2 * H,) + chunk, f32),
                jax.ShapeDtypeStruct((R, LANES), f32),
            ),
            in_specs=[pl.BlockSpec(memory_space=pltpu.HBM)] * 3,
            out_specs=(vmem, vmem),
            scratch_shapes=[
                pltpu.VMEM((n, LANES), bf16),
                pltpu.VMEM((k, LANES), bf16),
                pltpu.VMEM((k // LANES, LANES), f32),
                dma((3,)),
                pltpu.VMEM((k, 2 * LANES), bf16),
                pltpu.VMEM((k, n), bf16),
                pltpu.VMEM((n, 2 * LANES), bf16),
                pltpu.VMEM((k, COLS), f32),
                pltpu.VMEM((k, COLS), f32),
                pltpu.VMEM((R, LANES), f32),
                pltpu.VMEM((R, LANES), f32),
                pltpu.VMEM((C, R, LANES), f32),
                pltpu.VMEM((H,) + chunk, f32),
                pltpu.VMEM((H,) + chunk, f32),
                pltpu.VMEM((H,) + chunk, f32),
                pltpu.VMEM((max(X - 1, 1), H) + chunk, f32),
                dma((GROUPS, C)), dma((GROUPS, C)),
                dma((H,)), dma((H,)),
                dma((max(X - 1, 1), H)), dma((max(X - 1, 1), H)),
                dma((H,)), dma((H,)),
            ],
            compiler_params=pltpu.CompilerParams(
                collective_id=0, has_side_effects=True, vmem_limit_bytes=50 * 2**20
            ),
            cost_estimate=pl.CostEstimate(
                flops=8 * n * k * LANES, bytes_accessed=4 * n * LANES, transcendentals=n * k
            ),
        )(samples, centres, prior.reshape(k // LANES, LANES))
        new_centres = out[:, :CHUNK, :].reshape(k, LANES)
        new_log_prior = out[:, CHUNK:CHUNK + CHUNK // LANES, :].reshape(k)
        return new_centres, new_log_prior, lp.reshape(n)

    return jax.shard_map(
        shards,
        mesh=mesh,
        in_specs=(P("dp", None), P("centre", None), P("centre")),
        out_specs=(P("centre", None), P("centre"), P("dp")),
        check_vma=False,
    )
```

```python
import functools
import math

import jax
import jax.numpy as jnp
from jax import lax
from jax.experimental import pallas as pl
from jax.experimental.pallas import tpu as pltpu
from jax.sharding import PartitionSpec as P

MESH = pl.DeviceIdType.MESH
BETA = 0.0625
LANES = 128
COLS = 256
MOST = 256
GROUPS = 2


def pieces(value):
    first = value.astype(jnp.bfloat16)
    rest = value - first.astype(jnp.float32)
    second = rest.astype(jnp.bfloat16)
    third = (rest - second.astype(jnp.float32)).astype(jnp.bfloat16)
    return first, second, third


def side_columns(row):
    first, second, third = (p.astype(jnp.float32) for p in pieces(jnp.broadcast_to(row, (8, LANES))))
    line = lax.broadcasted_iota(jnp.int32, (8, LANES), 0)
    zero = jnp.zeros_like(first)
    eight = jnp.where(line == 0, first, jnp.where(line == 1, second, jnp.where(line == 2, third, zero)))
    rest = jnp.zeros((LANES - 8, LANES), jnp.float32)
    return jnp.concatenate([eight, rest], axis=0).T.astype(jnp.bfloat16)


def column(row):
    return jnp.broadcast_to(row, (LANES, LANES)).T


def unrolled(start, stop, body, most=4):
    width = math.gcd(stop - start, most)

    def step(i, unused):
        for u in range(width):
            body(start + i * width + u)
        return unused

    lax.fori_loop(0, (stop - start) // width, step, 0)


def kernel(
    C, D, x_hbm, c_hbm, p_hbm, out_ref, lp_ref, x_ref, c_ref, p_ref, in_sem,
    caug, e_ref, xw, score_a, score_b, m_ref, sn_ref, stats, own, send_a, recv_a, recv_b,
    stat_send, stat_recv, a_send, a_recv, b_send, b_recv, c_send, c_recv,
):
    n, k = x_ref.shape[0], c_ref.shape[0]
    X = D // 2
    CHUNK = min(MOST, k // 2)
    H = k // CHUNK // 2
    me_c, me_d = lax.axis_index("centre"), lax.axis_index("dp")
    core, mine_x = lax.rem(me_d, 2), lax.div(me_d, 2)
    sibling = mine_x * 2 + (1 - core)

    def far(q):
        return lax.rem(mine_x + q, X) * 2 + core

    p_copy = pltpu.make_async_copy(p_hbm, p_ref, in_sem.at[0])
    c_copy_in = pltpu.make_async_copy(c_hbm, c_ref, in_sem.at[1])
    x_copy = pltpu.make_async_copy(x_hbm, x_ref, in_sem.at[2])
    for copy in (p_copy, c_copy_in, x_copy):
        copy.start()

    barrier = pltpu.get_barrier_semaphore()

    def greet(q, unused):
        pl.semaphore_signal(
            barrier, inc=1, device_id={"centre": lax.rem(me_c + q, C)}, device_id_type=MESH
        )
        return unused

    lax.fori_loop(1, C, greet, 0)
    pl.semaphore_signal(barrier, inc=1, device_id={"dp": sibling}, device_id_type=MESH)
    for q in range(1, X):
        pl.semaphore_signal(barrier, inc=1, device_id={"dp": far(q)}, device_id_type=MESH)

    def widen(b):
        rows = pl.ds(pl.multiple_of(b * LANES, LANES), LANES)
        c = c_ref[rows, :].astype(jnp.float32)
        norm = jnp.sum((c * c).T, axis=0, keepdims=True)
        caug[rows, :LANES] = (c * (2.0 * BETA)).astype(jnp.bfloat16)
        caug[rows, LANES:] = side_columns(p_ref[pl.ds(b, 1), :] - norm * BETA)

    p_copy.wait()
    c_copy_in.wait()
    unrolled(0, k // LANES, widen)
    x_copy.wait()

    KB = min(512, k)
    steps = n // COLS
    ones = jnp.ones((COLS, LANES), jnp.bfloat16)

    def fold(s, op):
        return op(s.reshape(s.shape[0] // 8, 8, COLS), axis=0)

    def score_block(x_rows, kb):
        return lax.dot_general(
            caug[kb * KB:(kb + 1) * KB, :], x_rows, (((1,), (1,)), ((), ())),
            preferred_element_type=jnp.float32,
        )

    def x_of(j):
        rows = pl.ds(pl.multiple_of(j * COLS, COLS), COLS)
        return jnp.concatenate([x_ref[rows, :], ones], axis=1)

    def first_scores(ref, j):
        xr = x_of(j)
        top = None
        for kb in range(k // KB):
            s = score_block(xr, kb)
            ref[kb * KB:(kb + 1) * KB, :] = s
            part = fold(s, jnp.max)
            top = part if top is None else jnp.maximum(top, part)
        return jnp.max(top, axis=0, keepdims=True)

    def step(now, later, j, m):
        following = jnp.minimum(j + 1, steps - 1)
        xr = x_of(following)
        cols = pl.ds(pl.multiple_of(j * COLS, COLS), COLS)
        top = total = None
        for kb in range(k // KB):
            rows = slice(kb * KB, (kb + 1) * KB)
            s = score_block(xr, kb)
            later[rows, :] = s
            part = fold(s, jnp.max)
            top = part if top is None else jnp.maximum(top, part)
            e = jnp.exp(now[rows, :] - m)
            part = fold(e, jnp.sum)
            total = part if total is None else total + part
            e_ref[rows, cols] = e.astype(jnp.bfloat16)
        lse = m + jnp.log(jnp.sum(total, axis=0, keepdims=True))
        xf = x_ref[cols, :].astype(jnp.float32)
        norm = jnp.sum((xf * xf).T, axis=0, keepdims=True)
        for b in range(COLS // LANES):
            row = pl.ds(j * (COLS // LANES) + b, 1)
            part = slice(b * LANES, (b + 1) * LANES)
            m_ref[row, :] = m[:, part]
            sn_ref[row, :] = norm[:, part]
            stats[0, row, :] = lse[:, part]
        return jnp.max(top, axis=0, keepdims=True)

    def pair(i, m):
        m = step(score_a, score_b, 2 * i, m)
        return step(score_b, score_a, 2 * i + 1, m)

    R = n // LANES
    GR = R // GROUPS

    def stat_copy(g, q):
        rows = slice(g * GR, (g + 1) * GR)
        return pltpu.make_async_remote_copy(
            src_ref=stats.at[0, rows], dst_ref=stats.at[q, rows],
            send_sem=stat_send.at[g, q], recv_sem=stat_recv.at[g, q],
            device_id={"centre": lax.rem(me_c + q, C)}, device_id_type=MESH,
        )

    m = first_scores(score_a, 0)
    per_group = steps // 2 // GROUPS
    for g in range(GROUPS):
        m = lax.fori_loop(g * per_group, (g + 1) * per_group, pair, m)
        if g == 0:
            pl.semaphore_wait(barrier, C - 1 + 1 + X - 1)

        def send(q, unused, g=g):
            stat_copy(g, q).start()
            return unused

        lax.fori_loop(1, C, send, 0)

    for g in range(GROUPS):
        def arrive(q, unused, g=g):
            stat_copy(g, q).wait()
            return unused

        lax.fori_loop(1, C, arrive, 0)
        rows = slice(g * GR, (g + 1) * GR)
        top = lax.fori_loop(
            1, C, lambda q, t, rows=rows: jnp.maximum(t, stats[q, rows, :]), stats[0, rows, :]
        )
        total = lax.fori_loop(
            0, C, lambda q, t, rows=rows, top=top: t + jnp.exp(stats[q, rows, :] - top),
            jnp.zeros_like(top),
        )
        lse = top + jnp.log(total)
        lp_ref[rows, :] = lse - sn_ref[rows, :] * BETA
        m_ref[rows, :] = jnp.exp(m_ref[rows, :] - lse)

        def scale(r):
            at = pl.ds(pl.multiple_of(r * LANES, LANES), LANES)
            w = column(m_ref[pl.ds(r, 1), :])
            xw[at, :LANES] = (x_ref[at, :].astype(jnp.float32) * w).astype(jnp.bfloat16)
            xw[at, LANES:] = side_columns(m_ref[pl.ds(r, 1), :])

        unrolled(g * GR, (g + 1) * GR, scale)

    def partial(i):
        theirs, mine = (
            e_ref[pl.ds(pl.multiple_of((half * H + i) * CHUNK, CHUNK), CHUNK), :] for half in (1 - core, core)
        )
        both = jnp.dot(
            jnp.concatenate([theirs, mine], axis=0), xw[...], preferred_element_type=jnp.float32
        )
        line = lax.broadcasted_iota(jnp.int32, (8, LANES), 0)
        for ref, s in ((send_a, both[:CHUNK]), (own, both[CHUNK:])):
            ref[i, :CHUNK, :] = s[:, :LANES]
            masses = jnp.zeros((8, LANES), jnp.float32)
            for b in range(CHUNK // LANES):
                t = s[b * LANES:(b + 1) * LANES, LANES:].T
                row = jnp.sum(t[0:8, :], axis=0, keepdims=True)
                masses = jnp.where(line == b, jnp.broadcast_to(row, (8, LANES)), masses)
            ref[i, CHUNK:, :] = masses

    def a_copy(i):
        return pltpu.make_async_remote_copy(
            src_ref=send_a.at[i], dst_ref=recv_a.at[i], send_sem=a_send.at[i], recv_sem=a_recv.at[i],
            device_id={"dp": sibling}, device_id_type=MESH,
        )

    def b_copy(q, i):
        return pltpu.make_async_remote_copy(
            src_ref=own.at[i], dst_ref=recv_b.at[q - 1, i],
            send_sem=b_send.at[q - 1, i], recv_sem=b_recv.at[q - 1, i],
            device_id={"dp": far(q)}, device_id_type=MESH,
        )

    def c_copy(half, i):
        return pltpu.make_async_remote_copy(
            src_ref=out_ref.at[half * H + i], dst_ref=out_ref.at[half * H + i],
            send_sem=c_send.at[i], recv_sem=c_recv.at[i],
            device_id={"dp": sibling}, device_id_type=MESH,
        )

    def chip_sum(i):
        a_copy(i).wait()
        own[i] = own[i] + recv_a[i]
        for q in range(1, X):
            b_copy(q, i).start()

    def produce(i, unused):
        partial(i)
        a_copy(i).start()

        @pl.when(i > 0)
        def behind():
            chip_sum(i - 1)

        return unused

    lax.fori_loop(0, H, produce, 0)
    chip_sum(H - 1)

    denominator = float(n * D + k * C)

    def final(i, unused):
        chunk = core * H + i
        for q in range(1, X):
            b_copy(q, i).wait()
        parts = [own[i]] + [recv_b[q - 1, i] for q in range(1, X)]
        total = functools.reduce(lambda a, b: a + b, parts)
        for b in range(CHUNK // LANES):
            rows = pl.ds(pl.multiple_of(chunk * CHUNK, CHUNK) + b * LANES, LANES)
            mass = column(total[CHUNK + b:CHUNK + b + 1, :])
            c = c_ref[rows, :].astype(jnp.float32)
            out_ref[chunk, b * LANES:(b + 1) * LANES, :] = (
                total[b * LANES:(b + 1) * LANES, :] + c
            ) / (mass + 1.0)
        out_ref[chunk, CHUNK:, :] = jnp.log((total[CHUNK:, :] + 1.0) / denominator)
        c_copy(core, i).start()
        return unused

    lax.fori_loop(0, H, final, 0)

    def finish(i, unused):
        c_copy(core, i).wait()
        return unused

    lax.fori_loop(0, H, finish, 0)


def solution(mesh):
    C, D = mesh.shape["centre"], mesh.shape["dp"]

    def shards(samples, centres, prior):
        n, k = samples.shape[0], centres.shape[0]
        CHUNK = min(MOST, k // 2)
        X, H, R = D // 2, k // CHUNK // 2, n // LANES
        vmem = pl.BlockSpec(memory_space=pltpu.VMEM)
        f32, bf16 = jnp.float32, jnp.bfloat16
        dma = pltpu.SemaphoreType.DMA
        chunk = (CHUNK + 8, LANES)
        out, lp = pl.pallas_call(
            functools.partial(kernel, C, D),
            out_shape=(
                jax.ShapeDtypeStruct((2 * H,) + chunk, f32),
                jax.ShapeDtypeStruct((R, LANES), f32),
            ),
            in_specs=[pl.BlockSpec(memory_space=pltpu.HBM)] * 3,
            out_specs=(vmem, vmem),
            scratch_shapes=[
                pltpu.VMEM((n, LANES), bf16),
                pltpu.VMEM((k, LANES), bf16),
                pltpu.VMEM((k // LANES, LANES), f32),
                dma((3,)),
                pltpu.VMEM((k, 2 * LANES), bf16),
                pltpu.VMEM((k, n), bf16),
                pltpu.VMEM((n, 2 * LANES), bf16),
                pltpu.VMEM((k, COLS), f32),
                pltpu.VMEM((k, COLS), f32),
                pltpu.VMEM((R, LANES), f32),
                pltpu.VMEM((R, LANES), f32),
                pltpu.VMEM((C, R, LANES), f32),
                pltpu.VMEM((H,) + chunk, f32),
                pltpu.VMEM((H,) + chunk, f32),
                pltpu.VMEM((H,) + chunk, f32),
                pltpu.VMEM((max(X - 1, 1), H) + chunk, f32),
                dma((GROUPS, C)), dma((GROUPS, C)),
                dma((H,)), dma((H,)),
                dma((max(X - 1, 1), H)), dma((max(X - 1, 1), H)),
                dma((H,)), dma((H,)),
            ],
            compiler_params=pltpu.CompilerParams(
                collective_id=0, has_side_effects=True, vmem_limit_bytes=50 * 2**20
            ),
            cost_estimate=pl.CostEstimate(
                flops=8 * n * k * LANES, bytes_accessed=4 * n * LANES, transcendentals=n * k
            ),
        )(samples, centres, prior.reshape(k // LANES, LANES))
        new_centres = out[:, :CHUNK, :].reshape(k, LANES)
        new_log_prior = out[:, CHUNK:CHUNK + CHUNK // LANES, :].reshape(k)
        return new_centres, new_log_prior, lp.reshape(n)

    return jax.shard_map(
        shards,
        mesh=mesh,
        in_specs=(P("dp", None), P("centre", None), P("centre")),
        out_specs=(P("centre", None), P("centre"), P("dp")),
        check_vma=False,
    )
```

```python
import functools
import math

import jax
import jax.numpy as jnp
from jax import lax
from jax.experimental import pallas as pl
from jax.experimental.pallas import tpu as pltpu
from jax.sharding import PartitionSpec as P

MESH = pl.DeviceIdType.MESH
BETA = 0.0625
LANES = 128
COLS = 256
MOST = 256
GROUPS = 2


def pieces(value):
    first = value.astype(jnp.bfloat16)
    rest = value - first.astype(jnp.float32)
    second = rest.astype(jnp.bfloat16)
    third = (rest - second.astype(jnp.float32)).astype(jnp.bfloat16)
    return first, second, third


def side_columns(row):
    first, second, third = (p.astype(jnp.float32) for p in pieces(jnp.broadcast_to(row, (8, LANES))))
    line = lax.broadcasted_iota(jnp.int32, (8, LANES), 0)
    zero = jnp.zeros_like(first)
    eight = jnp.where(line == 0, first, jnp.where(line == 1, second, jnp.where(line == 2, third, zero)))
    rest = jnp.zeros((LANES - 8, LANES), jnp.float32)
    return jnp.concatenate([eight, rest], axis=0).T.astype(jnp.bfloat16)


def column(row):
    return jnp.broadcast_to(row, (LANES, LANES)).T


def unrolled(start, stop, body, most=4):
    width = math.gcd(stop - start, most)

    def step(i, unused):
        for u in range(width):
            body(start + i * width + u)
        return unused

    lax.fori_loop(0, (stop - start) // width, step, 0)


def kernel(
    C, D, x_hbm, c_hbm, p_hbm, out_ref, lp_ref, x_ref, c_ref, p_ref, in_sem,
    caug, e_ref, xw, score_a, score_b, m_ref, sn_ref, stats, own, send_a, recv_a, recv_b,
    stat_send, stat_recv, a_send, a_recv, b_send, b_recv, c_send, c_recv,
):
    n, k = x_ref.shape[0], c_ref.shape[0]
    X = D // 2
    CHUNK = min(MOST, k // 2)
    H = k // CHUNK // 2
    me_c, me_d = lax.axis_index("centre"), lax.axis_index("dp")
    core, mine_x = lax.rem(me_d, 2), lax.div(me_d, 2)
    sibling = mine_x * 2 + (1 - core)
    Q = C // 2
    half_c, par_c = lax.div(me_c, 2), lax.rem(me_c, 2)

    def peer(q):
        return jnp.where(q == 0, half_c * 2 + (1 - par_c), lax.rem(half_c + q, Q) * 2 + par_c)

    def far(q):
        return lax.rem(mine_x + q, X) * 2 + core

    p_copy = pltpu.make_async_copy(p_hbm, p_ref, in_sem.at[0])
    c_copy_in = pltpu.make_async_copy(c_hbm, c_ref, in_sem.at[1])
    x_copy = pltpu.make_async_copy(x_hbm, x_ref, in_sem.at[2])
    for copy in (p_copy, c_copy_in, x_copy):
        copy.start()

    barrier = pltpu.get_barrier_semaphore()

    def greet(q, unused):
        pl.semaphore_signal(
            barrier, inc=1, device_id={"centre": peer(q)}, device_id_type=MESH
        )
        return unused

    lax.fori_loop(0, Q, greet, 0)
    pl.semaphore_signal(barrier, inc=1, device_id={"dp": sibling}, device_id_type=MESH)
    for q in range(1, X):
        pl.semaphore_signal(barrier, inc=1, device_id={"dp": far(q)}, device_id_type=MESH)

    def widen(b):
        rows = pl.ds(pl.multiple_of(b * LANES, LANES), LANES)
        c = c_ref[rows, :].astype(jnp.float32)
        norm = jnp.sum((c * c).T, axis=0, keepdims=True)
        caug[rows, :LANES] = (c * (2.0 * BETA)).astype(jnp.bfloat16)
        caug[rows, LANES:] = side_columns(p_ref[pl.ds(b, 1), :] - norm * BETA)

    p_copy.wait()
    c_copy_in.wait()
    unrolled(0, k // LANES, widen)
    x_copy.wait()

    KB = min(512, k)
    steps = n // COLS
    ones = jnp.ones((COLS, LANES), jnp.bfloat16)

    def fold(s, op):
        return op(s.reshape(s.shape[0] // 8, 8, COLS), axis=0)

    def score_block(x_rows, kb):
        return lax.dot_general(
            caug[kb * KB:(kb + 1) * KB, :], x_rows, (((1,), (1,)), ((), ())),
            preferred_element_type=jnp.float32,
        )

    def x_of(j):
        rows = pl.ds(pl.multiple_of(j * COLS, COLS), COLS)
        return jnp.concatenate([x_ref[rows, :], ones], axis=1)

    def first_scores(ref, j):
        xr = x_of(j)
        top = None
        for kb in range(k // KB):
            s = score_block(xr, kb)
            ref[kb * KB:(kb + 1) * KB, :] = s
            part = fold(s, jnp.max)
            top = part if top is None else jnp.maximum(top, part)
        return jnp.max(top, axis=0, keepdims=True)

    def step(now, later, j, m):
        following = jnp.minimum(j + 1, steps - 1)
        xr = x_of(following)
        cols = pl.ds(pl.multiple_of(j * COLS, COLS), COLS)
        top = total = None
        for kb in range(k // KB):
            rows = slice(kb * KB, (kb + 1) * KB)
            s = score_block(xr, kb)
            later[rows, :] = s
            part = fold(s, jnp.max)
            top = part if top is None else jnp.maximum(top, part)
            e = jnp.exp(now[rows, :] - m)
            part = fold(e, jnp.sum)
            total = part if total is None else total + part
            e_ref[rows, cols] = e.astype(jnp.bfloat16)
        lse = m + jnp.log(jnp.sum(total, axis=0, keepdims=True))
        xf = x_ref[cols, :].astype(jnp.float32)
        norm = jnp.sum((xf * xf).T, axis=0, keepdims=True)
        for b in range(COLS // LANES):
            row = pl.ds(j * (COLS // LANES) + b, 1)
            part = slice(b * LANES, (b + 1) * LANES)
            m_ref[row, :] = m[:, part]
            sn_ref[row, :] = norm[:, part]
            stats[Q, row, :] = lse[:, part]
        return jnp.max(top, axis=0, keepdims=True)

    def pair(i, m):
        m = step(score_a, score_b, 2 * i, m)
        return step(score_b, score_a, 2 * i + 1, m)

    R = n // LANES
    GR = R // GROUPS

    def pair_copy(g):
        rows = slice(g * GR, (g + 1) * GR)
        return pltpu.make_async_remote_copy(
            src_ref=stats.at[Q, rows], dst_ref=stats.at[Q + 1, rows],
            send_sem=stat_send.at[g, 0], recv_sem=stat_recv.at[g, 0],
            device_id={"centre": half_c * 2 + (1 - par_c)}, device_id_type=MESH,
        )

    def stat_copy(g, q):
        rows = slice(g * GR, (g + 1) * GR)
        return pltpu.make_async_remote_copy(
            src_ref=stats.at[0, rows], dst_ref=stats.at[q, rows],
            send_sem=stat_send.at[g, q], recv_sem=stat_recv.at[g, q],
            device_id={"centre": lax.rem(half_c + q, Q) * 2 + par_c}, device_id_type=MESH,
        )

    def pass_on(g):
        pair_copy(g).wait()
        rows = slice(g * GR, (g + 1) * GR)
        mine, theirs = stats[Q, rows, :], stats[Q + 1, rows, :]
        top = jnp.maximum(mine, theirs)
        stats[0, rows, :] = top + jnp.log(jnp.exp(mine - top) + jnp.exp(theirs - top))

        def send(q, unused):
            stat_copy(g, q).start()
            return unused

        lax.fori_loop(1, Q, send, 0)

    m = first_scores(score_a, 0)
    per_group = steps // 2 // GROUPS
    for g in range(GROUPS):
        m = lax.fori_loop(g * per_group, (g + 1) * per_group, pair, m)
        if g == 0:
            pl.semaphore_wait(barrier, Q + X)
        pair_copy(g).start()
        if g > 0:
            pass_on(g - 1)
    pass_on(GROUPS - 1)

    for g in range(GROUPS):
        def arrive(q, unused, g=g):
            stat_copy(g, q).wait()
            return unused

        lax.fori_loop(1, Q, arrive, 0)
        rows = slice(g * GR, (g + 1) * GR)
        top = lax.fori_loop(
            1, Q, lambda q, t, rows=rows: jnp.maximum(t, stats[q, rows, :]), stats[0, rows, :]
        )
        total = lax.fori_loop(
            0, Q, lambda q, t, rows=rows, top=top: t + jnp.exp(stats[q, rows, :] - top),
            jnp.zeros_like(top),
        )
        lse = top + jnp.log(total)
        lp_ref[rows, :] = lse - sn_ref[rows, :] * BETA
        m_ref[rows, :] = jnp.exp(m_ref[rows, :] - lse)

        def scale(r):
            at = pl.ds(pl.multiple_of(r * LANES, LANES), LANES)
            w = column(m_ref[pl.ds(r, 1), :])
            xw[at, :LANES] = (x_ref[at, :].astype(jnp.float32) * w).astype(jnp.bfloat16)
            xw[at, LANES:] = side_columns(m_ref[pl.ds(r, 1), :])

        unrolled(g * GR, (g + 1) * GR, scale)

    def partial(i):
        theirs, mine = (
            e_ref[pl.ds(pl.multiple_of((half * H + i) * CHUNK, CHUNK), CHUNK), :] for half in (1 - core, core)
        )
        both = jnp.dot(
            jnp.concatenate([theirs, mine], axis=0), xw[...], preferred_element_type=jnp.float32
        )
        line = lax.broadcasted_iota(jnp.int32, (8, LANES), 0)
        for ref, s in ((send_a, both[:CHUNK]), (own, both[CHUNK:])):
            ref[i, :CHUNK, :] = s[:, :LANES]
            masses = jnp.zeros((8, LANES), jnp.float32)
            for b in range(CHUNK // LANES):
                t = s[b * LANES:(b + 1) * LANES, LANES:].T
                row = jnp.sum(t[0:8, :], axis=0, keepdims=True)
                masses = jnp.where(line == b, jnp.broadcast_to(row, (8, LANES)), masses)
            ref[i, CHUNK:, :] = masses

    def a_copy(i):
        return pltpu.make_async_remote_copy(
            src_ref=send_a.at[i], dst_ref=recv_a.at[i], send_sem=a_send.at[i], recv_sem=a_recv.at[i],
            device_id={"dp": sibling}, device_id_type=MESH,
        )

    def b_copy(q, i):
        return pltpu.make_async_remote_copy(
            src_ref=own.at[i], dst_ref=recv_b.at[q - 1, i],
            send_sem=b_send.at[q - 1, i], recv_sem=b_recv.at[q - 1, i],
            device_id={"dp": far(q)}, device_id_type=MESH,
        )

    def c_copy(half, i):
        return pltpu.make_async_remote_copy(
            src_ref=out_ref.at[half * H + i], dst_ref=out_ref.at[half * H + i],
            send_sem=c_send.at[i], recv_sem=c_recv.at[i],
            device_id={"dp": sibling}, device_id_type=MESH,
        )

    def chip_sum(i):
        a_copy(i).wait()
        own[i] = own[i] + recv_a[i]
        for q in range(1, X):
            b_copy(q, i).start()

    def produce(i, unused):
        partial(i)
        a_copy(i).start()

        @pl.when(i > 0)
        def behind():
            chip_sum(i - 1)

        return unused

    lax.fori_loop(0, H, produce, 0)
    chip_sum(H - 1)

    denominator = float(n * D + k * C)

    def final(i, unused):
        chunk = core * H + i
        for q in range(1, X):
            b_copy(q, i).wait()
        parts = [own[i]] + [recv_b[q - 1, i] for q in range(1, X)]
        total = functools.reduce(lambda a, b: a + b, parts)
        for b in range(CHUNK // LANES):
            rows = pl.ds(pl.multiple_of(chunk * CHUNK, CHUNK) + b * LANES, LANES)
            mass = column(total[CHUNK + b:CHUNK + b + 1, :])
            c = c_ref[rows, :].astype(jnp.float32)
            out_ref[chunk, b * LANES:(b + 1) * LANES, :] = (
                total[b * LANES:(b + 1) * LANES, :] + c
            ) / (mass + 1.0)
        out_ref[chunk, CHUNK:, :] = jnp.log((total[CHUNK:, :] + 1.0) / denominator)
        c_copy(core, i).start()
        return unused

    lax.fori_loop(0, H, final, 0)

    def finish(i, unused):
        c_copy(core, i).wait()
        return unused

    lax.fori_loop(0, H, finish, 0)


def solution(mesh):
    C, D = mesh.shape["centre"], mesh.shape["dp"]

    def shards(samples, centres, prior):
        n, k = samples.shape[0], centres.shape[0]
        CHUNK = min(MOST, k // 2)
        X, H, R = D // 2, k // CHUNK // 2, n // LANES
        vmem = pl.BlockSpec(memory_space=pltpu.VMEM)
        f32, bf16 = jnp.float32, jnp.bfloat16
        dma = pltpu.SemaphoreType.DMA
        chunk = (CHUNK + 8, LANES)
        out, lp = pl.pallas_call(
            functools.partial(kernel, C, D),
            out_shape=(
                jax.ShapeDtypeStruct((2 * H,) + chunk, f32),
                jax.ShapeDtypeStruct((R, LANES), f32),
            ),
            in_specs=[pl.BlockSpec(memory_space=pltpu.HBM)] * 3,
            out_specs=(vmem, vmem),
            scratch_shapes=[
                pltpu.VMEM((n, LANES), bf16),
                pltpu.VMEM((k, LANES), bf16),
                pltpu.VMEM((k // LANES, LANES), f32),
                dma((3,)),
                pltpu.VMEM((k, 2 * LANES), bf16),
                pltpu.VMEM((k, n), bf16),
                pltpu.VMEM((n, 2 * LANES), bf16),
                pltpu.VMEM((k, COLS), f32),
                pltpu.VMEM((k, COLS), f32),
                pltpu.VMEM((R, LANES), f32),
                pltpu.VMEM((R, LANES), f32),
                pltpu.VMEM((C // 2 + 2, R, LANES), f32),
                pltpu.VMEM((H,) + chunk, f32),
                pltpu.VMEM((H,) + chunk, f32),
                pltpu.VMEM((H,) + chunk, f32),
                pltpu.VMEM((max(X - 1, 1), H) + chunk, f32),
                dma((GROUPS, C // 2)), dma((GROUPS, C // 2)),
                dma((H,)), dma((H,)),
                dma((max(X - 1, 1), H)), dma((max(X - 1, 1), H)),
                dma((H,)), dma((H,)),
            ],
            compiler_params=pltpu.CompilerParams(
                collective_id=0, has_side_effects=True, vmem_limit_bytes=50 * 2**20
            ),
            cost_estimate=pl.CostEstimate(
                flops=8 * n * k * LANES, bytes_accessed=4 * n * LANES, transcendentals=n * k
            ),
        )(samples, centres, prior.reshape(k // LANES, LANES))
        new_centres = out[:, :CHUNK, :].reshape(k, LANES)
        new_log_prior = out[:, CHUNK:CHUNK + CHUNK // LANES, :].reshape(k)
        return new_centres, new_log_prior, lp.reshape(n)

    return jax.shard_map(
        shards,
        mesh=mesh,
        in_specs=(P("dp", None), P("centre", None), P("centre")),
        out_specs=(P("centre", None), P("centre"), P("dp")),
        check_vma=False,
    )
```

```python
import functools
import math

import jax
import jax.numpy as jnp
from jax import lax
from jax.experimental import pallas as pl
from jax.experimental.pallas import tpu as pltpu
from jax.sharding import PartitionSpec as P

MESH = pl.DeviceIdType.MESH
BETA = 0.0625
LANES = 128
COLS = 256
MOST = 128
GROUPS = 2


def pieces(value):
    first = value.astype(jnp.bfloat16)
    rest = value - first.astype(jnp.float32)
    second = rest.astype(jnp.bfloat16)
    third = (rest - second.astype(jnp.float32)).astype(jnp.bfloat16)
    return first, second, third


def side_columns(row):
    first, second, third = (p.astype(jnp.float32) for p in pieces(jnp.broadcast_to(row, (8, LANES))))
    line = lax.broadcasted_iota(jnp.int32, (8, LANES), 0)
    zero = jnp.zeros_like(first)
    eight = jnp.where(line == 0, first, jnp.where(line == 1, second, jnp.where(line == 2, third, zero)))
    rest = jnp.zeros((LANES - 8, LANES), jnp.float32)
    return jnp.concatenate([eight, rest], axis=0).T.astype(jnp.bfloat16)


def column(row):
    return jnp.broadcast_to(row, (LANES, LANES)).T


def unrolled(start, stop, body, most=4):
    width = math.gcd(stop - start, most)

    def step(i, unused):
        for u in range(width):
            body(start + i * width + u)
        return unused

    lax.fori_loop(0, (stop - start) // width, step, 0)


def kernel(
    C, D, x_hbm, c_hbm, p_hbm, out_ref, lp_ref, x_ref, c_ref, p_ref, in_sem,
    caug, e_ref, xw, score_a, score_b, m_ref, sn_ref, stats, own, send_a, recv_a, recv_b,
    stat_send, stat_recv, a_send, a_recv, b_send, b_recv, c_send, c_recv,
):
    n, k = x_ref.shape[0], c_ref.shape[0]
    X = D // 2
    CHUNK = min(MOST, k // 2)
    H = k // CHUNK // 2
    me_c, me_d = lax.axis_index("centre"), lax.axis_index("dp")
    core, mine_x = lax.rem(me_d, 2), lax.div(me_d, 2)
    sibling = mine_x * 2 + (1 - core)

    def far(q):
        return lax.rem(mine_x + q, X) * 2 + core

    p_copy = pltpu.make_async_copy(p_hbm, p_ref, in_sem.at[0])
    c_copy_in = pltpu.make_async_copy(c_hbm, c_ref, in_sem.at[1])
    x_copy = pltpu.make_async_copy(x_hbm, x_ref, in_sem.at[2])
    for copy in (p_copy, c_copy_in, x_copy):
        copy.start()

    barrier = pltpu.get_barrier_semaphore()

    def greet(q, unused):
        pl.semaphore_signal(
            barrier, inc=1, device_id={"centre": lax.rem(me_c + q, C)}, device_id_type=MESH
        )
        return unused

    lax.fori_loop(1, C, greet, 0)
    pl.semaphore_signal(barrier, inc=1, device_id={"dp": sibling}, device_id_type=MESH)
    for q in range(1, X):
        pl.semaphore_signal(barrier, inc=1, device_id={"dp": far(q)}, device_id_type=MESH)

    def widen(b):
        rows = pl.ds(pl.multiple_of(b * LANES, LANES), LANES)
        c = c_ref[rows, :].astype(jnp.float32)
        norm = jnp.sum((c * c).T, axis=0, keepdims=True)
        caug[rows, :LANES] = (c * (2.0 * BETA)).astype(jnp.bfloat16)
        caug[rows, LANES:] = side_columns(p_ref[pl.ds(b, 1), :] - norm * BETA)

    p_copy.wait()
    c_copy_in.wait()
    unrolled(0, k // LANES, widen)
    x_copy.wait()

    KB = min(512, k)
    steps = n // COLS
    ones = jnp.ones((COLS, LANES), jnp.bfloat16)

    def fold(s, op):
        return op(s.reshape(s.shape[0] // 8, 8, COLS), axis=0)

    def score_block(x_rows, kb):
        return lax.dot_general(
            caug[kb * KB:(kb + 1) * KB, :], x_rows, (((1,), (1,)), ((), ())),
            preferred_element_type=jnp.float32,
        )

    def x_of(j):
        rows = pl.ds(pl.multiple_of(j * COLS, COLS), COLS)
        return jnp.concatenate([x_ref[rows, :], ones], axis=1)

    def first_scores(ref, j):
        xr = x_of(j)
        top = None
        for kb in range(k // KB):
            s = score_block(xr, kb)
            ref[kb * KB:(kb + 1) * KB, :] = s
            part = fold(s, jnp.max)
            top = part if top is None else jnp.maximum(top, part)
        return jnp.max(top, axis=0, keepdims=True)

    def step(now, later, j, m):
        following = jnp.minimum(j + 1, steps - 1)
        xr = x_of(following)
        cols = pl.ds(pl.multiple_of(j * COLS, COLS), COLS)
        top = total = None
        for kb in range(k // KB):
            rows = slice(kb * KB, (kb + 1) * KB)
            s = score_block(xr, kb)
            later[rows, :] = s
            part = fold(s, jnp.max)
            top = part if top is None else jnp.maximum(top, part)
            e = jnp.exp(now[rows, :] - m)
            part = fold(e, jnp.sum)
            total = part if total is None else total + part
            e_ref[rows, cols] = e.astype(jnp.bfloat16)
        lse = m + jnp.log(jnp.sum(total, axis=0, keepdims=True))
        xf = x_ref[cols, :].astype(jnp.float32)
        norm = jnp.sum((xf * xf).T, axis=0, keepdims=True)
        for b in range(COLS // LANES):
            row = pl.ds(j * (COLS // LANES) + b, 1)
            part = slice(b * LANES, (b + 1) * LANES)
            m_ref[row, :] = m[:, part]
            sn_ref[row, :] = norm[:, part]
            stats[0, row, :] = lse[:, part]
        return jnp.max(top, axis=0, keepdims=True)

    def pair(i, m):
        m = step(score_a, score_b, 2 * i, m)
        return step(score_b, score_a, 2 * i + 1, m)

    R = n // LANES
    GR = R // GROUPS

    def stat_copy(g, q):
        rows = slice(g * GR, (g + 1) * GR)
        return pltpu.make_async_remote_copy(
            src_ref=stats.at[0, rows], dst_ref=stats.at[q, rows],
            send_sem=stat_send.at[g, q], recv_sem=stat_recv.at[g, q],
            device_id={"centre": lax.rem(me_c + q, C)}, device_id_type=MESH,
        )

    m = first_scores(score_a, 0)
    per_group = steps // 2 // GROUPS
    for g in range(GROUPS):
        m = lax.fori_loop(g * per_group, (g + 1) * per_group, pair, m)
        if g == 0:
            pl.semaphore_wait(barrier, C - 1 + 1 + X - 1)

        def send(q, unused, g=g):
            stat_copy(g, q).start()
            return unused

        lax.fori_loop(1, C, send, 0)

    for g in range(GROUPS):
        def arrive(q, unused, g=g):
            stat_copy(g, q).wait()
            return unused

        lax.fori_loop(1, C, arrive, 0)
        rows = slice(g * GR, (g + 1) * GR)
        top = lax.fori_loop(
            1, C, lambda q, t, rows=rows: jnp.maximum(t, stats[q, rows, :]), stats[0, rows, :]
        )
        total = lax.fori_loop(
            0, C, lambda q, t, rows=rows, top=top: t + jnp.exp(stats[q, rows, :] - top),
            jnp.zeros_like(top),
        )
        lse = top + jnp.log(total)
        lp_ref[rows, :] = lse - sn_ref[rows, :] * BETA
        m_ref[rows, :] = jnp.exp(m_ref[rows, :] - lse)

        def scale(r):
            at = pl.ds(pl.multiple_of(r * LANES, LANES), LANES)
            w = column(m_ref[pl.ds(r, 1), :])
            xw[at, :LANES] = (x_ref[at, :].astype(jnp.float32) * w).astype(jnp.bfloat16)
            xw[at, LANES:] = side_columns(m_ref[pl.ds(r, 1), :])

        unrolled(g * GR, (g + 1) * GR, scale)

    def partial(i):
        theirs, mine = (
            e_ref[pl.ds(pl.multiple_of((half * H + i) * CHUNK, CHUNK), CHUNK), :] for half in (1 - core, core)
        )
        both = jnp.dot(
            jnp.concatenate([theirs, mine], axis=0), xw[...], preferred_element_type=jnp.float32
        )
        line = lax.broadcasted_iota(jnp.int32, (8, LANES), 0)
        for ref, s in ((send_a, both[:CHUNK]), (own, both[CHUNK:])):
            ref[i, :CHUNK, :] = s[:, :LANES]
            masses = jnp.zeros((8, LANES), jnp.float32)
            for b in range(CHUNK // LANES):
                t = s[b * LANES:(b + 1) * LANES, LANES:].T
                row = jnp.sum(t[0:8, :], axis=0, keepdims=True)
                masses = jnp.where(line == b, jnp.broadcast_to(row, (8, LANES)), masses)
            ref[i, CHUNK:, :] = masses

    def a_copy(i):
        return pltpu.make_async_remote_copy(
            src_ref=send_a.at[i], dst_ref=recv_a.at[i], send_sem=a_send.at[i], recv_sem=a_recv.at[i],
            device_id={"dp": sibling}, device_id_type=MESH,
        )

    def b_copy(q, i):
        return pltpu.make_async_remote_copy(
            src_ref=own.at[i], dst_ref=recv_b.at[q - 1, i],
            send_sem=b_send.at[q - 1, i], recv_sem=b_recv.at[q - 1, i],
            device_id={"dp": far(q)}, device_id_type=MESH,
        )

    def c_copy(half, i):
        return pltpu.make_async_remote_copy(
            src_ref=out_ref.at[half * H + i], dst_ref=out_ref.at[half * H + i],
            send_sem=c_send.at[i], recv_sem=c_recv.at[i],
            device_id={"dp": sibling}, device_id_type=MESH,
        )

    def chip_sum(i):
        a_copy(i).wait()
        own[i] = own[i] + recv_a[i]
        for q in range(1, X):
            b_copy(q, i).start()

    def produce(i, unused):
        partial(i)
        a_copy(i).start()

        @pl.when(i > 0)
        def behind():
            chip_sum(i - 1)

        return unused

    lax.fori_loop(0, H, produce, 0)
    chip_sum(H - 1)

    denominator = float(n * D + k * C)

    def final(i, unused):
        chunk = core * H + i
        for q in range(1, X):
            b_copy(q, i).wait()
        parts = [own[i]] + [recv_b[q - 1, i] for q in range(1, X)]
        total = functools.reduce(lambda a, b: a + b, parts)
        for b in range(CHUNK // LANES):
            rows = pl.ds(pl.multiple_of(chunk * CHUNK, CHUNK) + b * LANES, LANES)
            mass = column(total[CHUNK + b:CHUNK + b + 1, :])
            c = c_ref[rows, :].astype(jnp.float32)
            out_ref[chunk, b * LANES:(b + 1) * LANES, :] = (
                total[b * LANES:(b + 1) * LANES, :] + c
            ) / (mass + 1.0)
        out_ref[chunk, CHUNK:, :] = jnp.log((total[CHUNK:, :] + 1.0) / denominator)
        c_copy(core, i).start()
        return unused

    lax.fori_loop(0, H, final, 0)

    def finish(i, unused):
        c_copy(core, i).wait()
        return unused

    lax.fori_loop(0, H, finish, 0)


def solution(mesh):
    C, D = mesh.shape["centre"], mesh.shape["dp"]

    def shards(samples, centres, prior):
        n, k = samples.shape[0], centres.shape[0]
        CHUNK = min(MOST, k // 2)
        X, H, R = D // 2, k // CHUNK // 2, n // LANES
        vmem = pl.BlockSpec(memory_space=pltpu.VMEM)
        f32, bf16 = jnp.float32, jnp.bfloat16
        dma = pltpu.SemaphoreType.DMA
        chunk = (CHUNK + 8, LANES)
        out, lp = pl.pallas_call(
            functools.partial(kernel, C, D),
            out_shape=(
                jax.ShapeDtypeStruct((2 * H,) + chunk, f32),
                jax.ShapeDtypeStruct((R, LANES), f32),
            ),
            in_specs=[pl.BlockSpec(memory_space=pltpu.HBM)] * 3,
            out_specs=(vmem, vmem),
            scratch_shapes=[
                pltpu.VMEM((n, LANES), bf16),
                pltpu.VMEM((k, LANES), bf16),
                pltpu.VMEM((k // LANES, LANES), f32),
                dma((3,)),
                pltpu.VMEM((k, 2 * LANES), bf16),
                pltpu.VMEM((k, n), bf16),
                pltpu.VMEM((n, 2 * LANES), bf16),
                pltpu.VMEM((k, COLS), f32),
                pltpu.VMEM((k, COLS), f32),
                pltpu.VMEM((R, LANES), f32),
                pltpu.VMEM((R, LANES), f32),
                pltpu.VMEM((C, R, LANES), f32),
                pltpu.VMEM((H,) + chunk, f32),
                pltpu.VMEM((H,) + chunk, f32),
                pltpu.VMEM((H,) + chunk, f32),
                pltpu.VMEM((max(X - 1, 1), H) + chunk, f32),
                dma((GROUPS, C)), dma((GROUPS, C)),
                dma((H,)), dma((H,)),
                dma((max(X - 1, 1), H)), dma((max(X - 1, 1), H)),
                dma((H,)), dma((H,)),
            ],
            compiler_params=pltpu.CompilerParams(
                collective_id=0, has_side_effects=True, vmem_limit_bytes=50 * 2**20
            ),
            cost_estimate=pl.CostEstimate(
                flops=8 * n * k * LANES, bytes_accessed=4 * n * LANES, transcendentals=n * k
            ),
        )(samples, centres, prior.reshape(k // LANES, LANES))
        new_centres = out[:, :CHUNK, :].reshape(k, LANES)
        new_log_prior = out[:, CHUNK:CHUNK + CHUNK // LANES, :].reshape(k)
        return new_centres, new_log_prior, lp.reshape(n)

    return jax.shard_map(
        shards,
        mesh=mesh,
        in_specs=(P("dp", None), P("centre", None), P("centre")),
        out_specs=(P("centre", None), P("centre"), P("dp")),
        check_vma=False,
    )
```
